32 devices in a mesh: cell: 4 (over y, x), gene: 8 (over z, core).
Axes of the slice: x: 2, y: 2, z: 4, core: 2. Of those that a mesh axis runs over, the one named last changes fastest.
Arguments:
- expression: bfloat16 [4096, 15360], P('cell', 'gene'), may hold values from -12 to 12
- prior_values: bfloat16 [15360, 1792], P('gene'), may hold values from -0.078125 to 0.078125
- block_mask: int32 [120, 14], P('gene'), may hold values 0 or 1
- gram_inverse: bfloat16 [1792, 1792], P(None, 'gene'), may hold values from -1 to 2
Outputs:
- coefficients: float32 [1792, 15360], P('cell', 'gene')
The draws below stay inside these ranges and needn't reach their ends.
All inputs are finite; a program needn't handle non-finite values. No bound on the sum of `block_mask` on one device may be relied on, other than what follows from the above.
Results may differ from the reference program's by a relative error of at most 0.025.
Values may be sent and summed in bfloat16 or wider, within the bound.
No kernel may reach another device: no remote copies, remote signals or barrier semaphores. Data moves between devices by JAX's collectives and lax.ppermute only.
A program may use at most 128 MiB of HBM per device.

```python
import jax
import jax.numpy as jnp
from jax import lax

F = 1792
BLOCK = 128
CELL_DEV = 1024
ITERS = 2
CELLS = 4096
GENES = 15360
N_CELL = 4


def draw_gram_inverse(key, part):
    noise = jnp.clip(jax.random.normal(jax.random.fold_in(key, 17), (F, F), jnp.float32), -4.0, 4.0)
    matrix = jnp.eye(F, dtype=jnp.float32) + 0.5 * noise / jnp.sqrt(jnp.float32(F))
    return matrix.astype(jnp.bfloat16)


def draw_expression(key, part):
    position = (jnp.arange(CELLS, dtype=jnp.float32) + 0.5) / CELLS
    values = jnp.clip(jax.random.normal(jax.random.fold_in(key, 23), (CELLS, GENES), jnp.float32), -4.0, 4.0)
    row_scale = jnp.exp(jnp.log(8.0) * (position - 0.5))
    field = values * row_scale[:, None]
    return field.astype(jnp.bfloat16)


def touch_ends(entries, stream_key, least, largest):
    spot = [jax.random.randint(jax.random.fold_in(stream_key, axis), (), 0, length) for axis, length in enumerate(entries.shape)]
    main_axis = entries.shape.index(max(entries.shape))
    neighbour = spot[:main_axis] + [(spot[main_axis] + 1) % entries.shape[main_axis]] + spot[main_axis + 1:]
    return entries.at[tuple(spot)].set(least).at[tuple(neighbour)].set(largest)


def block_levels(stream_key, shape, split, low, top_value):
    factor_of = 1.0
    for dim, parts in split:
        heights = jax.random.uniform(jax.random.fold_in(jax.random.fold_in(stream_key, 6), dim), (parts,), jnp.float32, low / len(split), top_value / len(split))
        factor_of = factor_of * jnp.repeat(jnp.exp(heights), shape[dim] // parts).reshape((-1,) + (1,) * (len(shape) - 1 - dim))
    return factor_of


def gaussian(stream_key, dims, width, bound, pieces=(), held_as=jnp.bfloat16):
    loudness = block_levels(stream_key, dims, pieces, -0.22, 0.18) if pieces else 1.0
    drawn = jax.random.normal(stream_key, dims, jnp.float32) * width * loudness
    return jnp.minimum(jnp.maximum(drawn, -bound), bound).astype(held_as)


def setup_inputs(seed: int = 0) -> dict:
    key_of = jax.random.split(jax.random.key(seed), 5)
    expression = draw_expression(jax.random.fold_in(key_of[4], 71), 0)
    prior_values = gaussian(key_of[1], (GENES, F), (GENES // 3) ** -0.5, 0.078125, ((0, 8),))
    block_mask = touch_ends((jax.random.randint(key_of[2], (GENES // BLOCK, F // BLOCK), 0, 3) < 1).astype(jnp.int32), jax.random.fold_in(key_of[2], 1), 0, 1)
    gram_inverse = draw_gram_inverse(jax.random.fold_in(key_of[4], 71), 0)
    return {"expression": expression, "prior_values": prior_values, "block_mask": block_mask, "gram_inverse": gram_inverse}


OUT_UNITS = 100.0
LASSO = 0.006
RIDGE = 0.1
PRIOR_RELIEF = 0.7
EPSILON = 1e-6


def shrink(moved, limit, step_size):
    kept = jnp.maximum(moved - limit, 0.0) - jnp.maximum(-moved - limit, 0.0)
    return kept / (1.0 + step_size * RIDGE)


def reference(expression, prior_values, block_mask, gram_inverse):
    support = jnp.repeat(jnp.repeat(block_mask.astype(jnp.float32), BLOCK, axis=0), BLOCK, axis=1)
    masked = (prior_values.astype(jnp.float32) * support).astype(jnp.bfloat16)
    tf_scores = jnp.dot(expression, masked, preferred_element_type=jnp.float32).astype(jnp.bfloat16)
    activity = jnp.dot(tf_scores, gram_inverse, preferred_element_type=jnp.float32).astype(jnp.bfloat16)
    widened = activity.astype(jnp.float32)
    sum_squares = jnp.sum(widened * widened)
    step_size = 0.5 / (sum_squares / (CELLS * F) + EPSILON)
    limit = step_size * LASSO * (1.0 - PRIOR_RELIEF * support.T)
    coefficient = jnp.zeros((F, GENES), jnp.float32)
    blocked_activity = activity.reshape(N_CELL, CELL_DEV, F)

    def add_block(carried, pair):
        product = jnp.dot(pair[0].T, pair[1], preferred_element_type=jnp.float32)
        rounded = lax.optimization_barrier(product.astype(jnp.bfloat16))
        return carried + rounded.astype(jnp.float32), None

    for sweep in range(ITERS):
        if sweep == 0:
            residual = -expression
        else:
            fitted = jnp.dot(activity, coefficient.astype(jnp.bfloat16), preferred_element_type=jnp.float32)
            residual = (fitted - expression.astype(jnp.float32)).astype(jnp.bfloat16)
        blocked_residual = residual.reshape(N_CELL, CELL_DEV, GENES)
        summed, unused = lax.scan(add_block, jnp.zeros((F, GENES), jnp.float32), (blocked_activity, blocked_residual))
        gradient = summed / CELLS
        coefficient = shrink(coefficient - step_size * gradient, limit, step_size)
    return coefficient * OUT_UNITS
```

```python
import jax
import jax.numpy as jnp
from jax import lax
from jax.sharding import PartitionSpec as P

BLOCK = 128
CORES = 2
OUT_UNITS = 100.0
LASSO = 0.006
RIDGE = 0.1
PRIOR_RELIEF = 0.7
EPSILON = 1e-06


def shrink(moved, limit, step_size):
    kept = jnp.maximum(moved - limit, 0.0) - jnp.maximum(-moved - limit, 0.0)
    return kept / (1.0 + step_size * RIDGE)


def cell_swap(x, mask):
    n = lax.axis_size("cell")
    return lax.ppermute(x, "cell", [(i, i ^ mask) for i in range(n)])


def core_swap(x):
    n = lax.axis_size("gene")
    return lax.ppermute(x, "gene", [(i, i ^ 1) for i in range(n)])


def chip_shift(x, r):
    n = lax.axis_size("gene")
    return lax.ppermute(x, "gene", [(i, (i + CORES * r) % n) for i in range(n)])


def on_device(expression, prior_values, block_mask, gram_inverse):
    bf16, f32 = jnp.bfloat16, jnp.float32
    n_cell, n_gene = lax.axis_size("cell"), lax.axis_size("gene")
    n_chip = n_gene // CORES
    me_cell, me_gene = lax.axis_index("cell"), lax.axis_index("gene")
    chip, core = me_gene // CORES, me_gene % CORES
    cells, genes = expression.shape
    factors = prior_values.shape[1]
    gene_blocks, factor_blocks = block_mask.shape
    piece = cells // n_gene
    total_cells = cells * n_cell
    masks = list(range(n_cell))

    wide_blocks = -(-gene_blocks // n_cell)
    wide = wide_blocks * BLOCK

    def first_block(j):
        return jnp.minimum(j * wide_blocks, gene_blocks - wide_blocks)

    gram_t = gram_inverse.T
    share = gram_t.shape[0] // n_cell
    own_share = lax.dynamic_slice_in_dim(gram_t, me_cell * share, share, 0)
    over_chips = [own_share] + [chip_shift(own_share, r) for r in range(1, n_chip)]
    over_chips = jnp.stack(over_chips)
    over_cells = jnp.stack([over_chips] + [cell_swap(over_chips, m) for m in masks[1:]])
    other_core = core_swap(over_cells)
    both = jnp.stack([over_cells, other_core])

    rows = expression.reshape(n_chip, CORES, piece, genes)

    def rows_of(r, s):
        z = lax.rem(chip - r + n_chip, n_chip)
        return lax.dynamic_slice(rows, (z, core ^ s, 0, 0), (1, 1, piece, genes))[0, 0]

    near = jnp.concatenate([rows_of(r, 0) for r in range(n_chip)])
    far = jnp.concatenate([rows_of(r, 1) for r in range(n_chip)])

    support = block_mask.astype(bf16)[:, None, :, None]
    masked = (prior_values.reshape(gene_blocks, BLOCK, factor_blocks, BLOCK) * support).reshape(
        genes, factors
    )
    far_scores = jnp.dot(far, masked, preferred_element_type=f32).astype(bf16)
    from_core = core_swap(far_scores)
    near_scores = jnp.dot(near, masked, preferred_element_type=f32)
    chip_scores = (near_scores + from_core.astype(f32)).astype(bf16)
    chip_scores = chip_scores.reshape(n_chip, piece, factors)
    scores = chip_scores[0].astype(f32)
    for r in range(1, n_chip):
        scores = scores + chip_shift(chip_scores[r], -r).astype(f32)
    scores = scores.astype(bf16)

    def columns_for(j, part):
        return lax.dynamic_slice_in_dim(part, first_block(j) * BLOCK, wide, 1)

    def exchange(part):
        out = []
        for m in masks:
            send = columns_for(me_cell ^ m, part)
            out.append(send if m == 0 else cell_swap(send, m))
        return out

    expr = [exchange(near), exchange(far)]

    act = lax.dot_general(
        both.reshape(factors, factors), scores, (((1,), (1,)), ((), ())), preferred_element_type=f32
    ).astype(bf16)
    act = act.reshape(CORES, n_cell, n_chip, share, piece)
    act = jnp.where(core == 0, act, act[::-1])
    act = jnp.stack([lax.dynamic_index_in_dim(act, me_cell ^ j, 1, False) for j in masks], 1)
    act = jnp.stack(
        [
            lax.dynamic_index_in_dim(act, lax.rem(chip - z + n_chip, n_chip), 2, False)
            for z in range(n_chip)
        ],
        0,
    )
    act = act.reshape(factors, piece)

    parts, exprs = [], []
    for r in range(n_chip):
        mine = act if r == 0 else chip_shift(act, r)
        near_parts = [mine] + [cell_swap(mine, m) for m in masks[1:]]
        near_part = jnp.concatenate(near_parts, 1)
        far_part = core_swap(near_part)
        parts.append(jnp.concatenate([near_part, far_part], 1))
        exprs.append(
            jnp.concatenate(
                [expr[s][m][r * piece : (r + 1) * piece] for s in range(CORES) for m in masks]
            )
        )

    sum_squares = sum(jnp.sum(jnp.square(p.astype(f32))) for p in parts)
    step_size = 0.5 / (sum_squares / (total_cells * factors) + EPSILON)
    own_blocks = lax.dynamic_slice_in_dim(block_mask, first_block(me_cell), wide_blocks, 0)
    relief = own_blocks.T.astype(f32)[:, None, :, None]
    penalty = jnp.broadcast_to(
        1.0 - PRIOR_RELIEF * relief, (factor_blocks, BLOCK, wide_blocks, BLOCK)
    ).reshape(factors, wide)
    limit = step_size * LASSO * penalty

    gradient = sum(jnp.dot(a, e, preferred_element_type=f32) for a, e in zip(parts, exprs))
    coefficient = shrink(step_size * (gradient / total_cells), limit, step_size)
    coefficient_bf = coefficient.astype(bf16)
    residuals = []
    for a, e in zip(parts, exprs):
        fitted = lax.dot_general(
            a, coefficient_bf, (((0,), (0,)), ((), ())), preferred_element_type=f32
        )
        residuals.append((fitted - e.astype(f32)).astype(bf16))

    tf_rows = factors // n_cell
    arrived = {}
    for m in masks[::-1]:
        first = (me_cell ^ m) * tf_rows
        cut = lambda x: lax.dynamic_slice_in_dim(x, first, tf_rows, 0)
        gradient = sum(
            jnp.dot(cut(a), b, preferred_element_type=f32) for a, b in zip(parts, residuals)
        )
        moved = cut(coefficient) - step_size * (gradient / total_cells)
        done = shrink(moved, cut(limit), step_size)
        arrived[m] = done.astype(bf16) if m == 0 else cell_swap(done.astype(bf16), m)
    stacked = jnp.stack([arrived[m] for m in masks])
    columns = []
    for j in range(n_cell):
        block = lax.dynamic_index_in_dim(stacked, me_cell ^ j, 0, False)
        overlap = max(0, (j + 1) * wide_blocks - gene_blocks) * BLOCK
        columns.append(block[:, overlap:])
    return jnp.concatenate(columns, 1).astype(f32) * OUT_UNITS


def solution(mesh):
    in_specs = (P("cell", "gene"), P("gene", None), P("gene", None), P(None, "gene"))
    out_specs = P("cell", "gene")
    return jax.shard_map(
        on_device, mesh=mesh, in_specs=in_specs, out_specs=out_specs, check_vma=False
    )
```

```python
import jax
import jax.numpy as jnp
from jax import lax
from jax.experimental import pallas as pl
from jax.experimental.pallas import tpu as pltpu
from jax.sharding import PartitionSpec as P

BLOCK = 128
CORES = 2
ROWS = 16
SCOPED = 2 << 20
OUT_UNITS = 100.0
LASSO = 0.006
RIDGE = 0.1
PRIOR_RELIEF = 0.7
EPSILON = 1e-06

bf16, f32 = jnp.bfloat16, jnp.float32
ANYWHERE = pl.BlockSpec(memory_space=pl.ANY)


def shrink(moved, limit, step_size):
    kept = jnp.maximum(moved - limit, 0.0) - jnp.maximum(-moved - limit, 0.0)
    return kept / (1.0 + step_size * RIDGE)


def cell_swap(x, mask):
    n = lax.axis_size("cell")
    return lax.ppermute(x, "cell", [(i, i ^ mask) for i in range(n)])


def core_swap(x):
    n = lax.axis_size("gene")
    return lax.ppermute(x, "gene", [(i, i ^ 1) for i in range(n)])


def chip_swap(x, mask):
    n = lax.axis_size("gene")
    return lax.ppermute(x, "gene", [(i, i ^ (CORES * mask)) for i in range(n)])


def after(x, *others):
    return pl.pallas_call(
        lambda *refs: None,
        in_specs=[ANYWHERE] * (1 + len(others)),
        out_specs=ANYWHERE,
        out_shape=jax.ShapeDtypeStruct(x.shape, x.dtype),
        input_output_aliases={0: 0},
        compiler_params=pltpu.CompilerParams(vmem_limit_bytes=SCOPED),
        name="after",
    )(x, *others)


def collect(sources, moves, shapes, starts=None, others=()):
    starts = jnp.zeros((1,), jnp.int32) if starts is None else starts.astype(jnp.int32)
    n, n_out = len(sources), len(shapes)

    def kernel(starts_ref, *refs):
        outs = refs[n + len(others) : n + len(others) + n_out]
        sems = refs[-1]

        def view(ref, slices):
            at = []
            for start, size in slices:
                if isinstance(start, tuple):
                    start = pl.multiple_of(starts_ref[start[0]] * start[1], start[1])
                at.append(pl.ds(start, size))
            return ref.at[tuple(at)]

        def copy(i):
            _, source, taken, out, put = moves[i]
            return pltpu.make_async_copy(view(refs[source], taken), view(outs[out], put), sems.at[i])

        def each(act):
            for i, (condition, *_) in enumerate(moves):
                if condition is None:
                    act(copy(i))
                else:
                    index, value = condition
                    pl.when(starts_ref[index] == value)(lambda i=i: act(copy(i)))

        each(lambda c: c.start())
        each(lambda c: c.wait())

    sources = [pltpu.with_memory_space_constraint(x, pltpu.HBM) for x in sources]
    return pl.pallas_call(
        kernel,
        in_specs=[pl.BlockSpec(memory_space=pltpu.SMEM)] + [ANYWHERE] * (n + len(others)),
        out_specs=[ANYWHERE] * n_out,
        out_shape=[pltpu.VMEM(shape, bf16) for shape in shapes],
        scratch_shapes=[pltpu.SemaphoreType.DMA((len(moves),))],
        compiler_params=pltpu.CompilerParams(vmem_limit_bytes=SCOPED),
        name="collect",
    )(starts, *sources, *others)


def join(pieces, axis, others=()):
    if any(x.shape[axis] % (BLOCK if axis else ROWS) for x in pieces):
        return after(jnp.concatenate(pieces, axis), *others)
    moves, at = [], 0
    for i, x in enumerate(pieces):
        taken = [(0, size) for size in x.shape]
        put = list(taken)
        put[axis] = (at, x.shape[axis])
        moves.append((None, i, taken, 0, put))
        at += x.shape[axis]
    shape = list(pieces[0].shape)
    shape[axis] = at
    return collect(pieces, moves, [tuple(shape)], others=others)[0]


def masked_prior(prior_values, block_mask, others):
    gene_blocks, factor_blocks = block_mask.shape

    def kernel(mask_ref, prior_ref, *refs):
        out_ref, sems = refs[-2:]

        def copy(i):
            rows = pl.ds(pl.multiple_of(i * BLOCK, BLOCK), BLOCK)
            return pltpu.make_async_copy(prior_ref.at[rows], out_ref.at[rows], sems.at[i])

        @pl.loop(0, gene_blocks)
        def _(i):
            copy(i).start()

        @pl.loop(0, gene_blocks)
        def _(i):
            copy(i).wait()
            for j in range(factor_blocks):

                @pl.when(mask_ref[i, j] == 0)
                def _():
                    rows = pl.ds(pl.multiple_of(i * BLOCK, BLOCK), BLOCK)
                    out_ref[rows, j * BLOCK : (j + 1) * BLOCK] = jnp.zeros((BLOCK, BLOCK), bf16)

    return pl.pallas_call(
        kernel,
        in_specs=[pl.BlockSpec(memory_space=pltpu.SMEM)] + [ANYWHERE] * (1 + len(others)),
        out_specs=pl.BlockSpec(memory_space=pltpu.VMEM),
        out_shape=pltpu.VMEM(prior_values.shape, bf16),
        scratch_shapes=[pltpu.SemaphoreType.DMA((gene_blocks,))],
        compiler_params=pltpu.CompilerParams(vmem_limit_bytes=12 << 20),
        name="masked",
    )(block_mask, pltpu.with_memory_space_constraint(prior_values, pltpu.HBM), *others)


def cell_gather(x, axis):
    n = lax.axis_size("cell")
    half = x.shape[axis] // 2
    got = [[x]]
    for m in range(1, n):
        low = m & -m
        high = m ^ low
        if not high:
            got.append([cell_swap(x, m)])
            continue

        def half_of(pieces, i):
            if len(pieces) == 2:
                return pieces[i]
            return lax.slice_in_dim(pieces[0], i * half, (i + 1) * half, axis=axis)

        first = cell_swap(half_of(got[high], 0), low)
        second = half_of(got[low], 1)
        for bit in range(n.bit_length()):
            if high >> bit & 1:
                second = cell_swap(second, 1 << bit)
        got.append([first, second])
    return [piece for pieces in got for piece in pieces]


def on_device(expression, prior_values, block_mask, gram_inverse):
    n_cell, n_gene = lax.axis_size("cell"), lax.axis_size("gene")
    n_chip = n_gene // CORES
    me_cell, me_gene = lax.axis_index("cell"), lax.axis_index("gene")
    chip, core = me_gene // CORES, me_gene % CORES
    cells, genes = expression.shape
    factors = prior_values.shape[1]
    gene_blocks, factor_blocks = block_mask.shape
    piece = cells // n_gene
    total_cells = cells * n_cell
    masks = list(range(n_cell))
    several = [m for m in masks if m & (m - 1)]
    single = [m for m in masks if m and m not in several]

    wide_blocks = -(-gene_blocks // n_cell)
    wide = wide_blocks * BLOCK

    def first_block(j):
        return jnp.minimum(j * wide_blocks, gene_blocks - wide_blocks)

    width = gram_inverse.shape[1]
    share = -(-width // (ROWS * n_cell)) * ROWS

    def share_start(j):
        return jnp.minimum(j * share, width - share)

    gram_share = lax.dynamic_slice_in_dim(gram_inverse.T, share_start(me_cell), share, 0)
    chip_order = [0]
    bits = [1 << i for i in reversed(range(n_chip.bit_length() - 1))]
    for bit in bits:
        chip_order += [z ^ bit for z in chip_order]

    def columns_of(starts, m):
        return lax.dynamic_slice_in_dim(expression, starts[m], wide, 1)

    starts = jnp.stack([first_block(me_cell ^ m) * BLOCK for m in masks]).astype(jnp.int32)
    columns = {m: columns_of(starts, m) for m in single}
    swapped = {m: cell_swap(columns[m], m) for m in single}

    masked = masked_prior(prior_values, block_mask, list(columns.values()))

    def rows_of(core_index, others):
        moves = [
            (None, 0, [((z, piece), piece), (0, genes)], 0, [(z * piece, piece), (0, genes)])
            for z in range(n_chip)
        ]
        places = jnp.stack([z * CORES + core_index for z in range(n_chip)])
        return collect([expression], moves, [(n_chip * piece, genes)], places, others)[0]

    far_scores = jnp.dot(
        rows_of(core ^ 1, list(columns.values())), masked, preferred_element_type=f32
    ).astype(bf16)
    shares = after(gram_share, far_scores)
    for bit in bits[:-1]:
        shares = jnp.concatenate([shares, chip_swap(shares, bit)])
    near_scores = jnp.dot(rows_of(core, [far_scores]), masked, preferred_element_type=f32)
    chip_scores = (near_scores + core_swap(far_scores).astype(f32)).astype(bf16)
    chip_scores = chip_scores.reshape(n_chip, piece, factors)
    scores = lax.dynamic_index_in_dim(chip_scores, chip, 0, False).astype(f32)
    givens = [lax.dynamic_index_in_dim(chip_scores, chip ^ z, 0, False) for z in range(1, n_chip)]
    for z, given in enumerate(givens):
        scores = scores + chip_swap(given, z + 1).astype(f32)
    scores = scores.astype(bf16)

    shares = after(shares, chip_scores, *givens)
    shares = jnp.concatenate([shares, chip_swap(shares, 1)])
    shares = cell_gather(after(shares, *swapped.values()), 0)
    near_gram = join(shares, 0)
    far_gram = join([core_swap(x) for x in shares], 0)
    starts = after(starts, near_gram)
    columns = {m: columns_of(starts, m) for m in [0] + several}
    swapped.update({m: cell_swap(columns[m], m) for m in several})
    expr = [columns[0]] + [swapped[m] for m in masks[1:]]
    halves = [
        lax.dot_general(
            gram, scores, (((1,), (1,)), ((), ())), preferred_element_type=f32
        ).astype(bf16)
        for gram in (near_gram, far_gram)
    ]
    moves, places = [], []
    for s in range(CORES):
        for m in masks:
            for i, z in enumerate(chip_order):
                from_row = (m * n_chip + i) * share
                j = me_cell ^ m
                first = ((chip ^ z) * CORES + (core ^ s)) * width
                at = len(places)
                places += [(first + j * share) // ROWS, j]
                for value in masks:
                    size = min(share, width - value * share)
                    if size > 0:
                        taken = [(from_row + share - size, size), (0, piece)]
                        moves.append(
                            ((at + 1, value), s, taken, 0, [((at, ROWS), size), (0, piece)])
                        )
    act = collect(halves, moves, [(factors, piece)], jnp.stack(places))[0]

    squares = jnp.sum(jnp.square(act.astype(f32)), keepdims=True)
    squares = jnp.broadcast_to(squares, (8, BLOCK))
    squares = squares + core_swap(squares)
    for bit in bits:
        squares = squares + chip_swap(squares, bit)
    for m in single:
        squares = squares + cell_swap(squares, m)

    own = [act]
    for z in range(1, n_chip):
        low = z & -z
        own.append(chip_swap(own[z ^ low], low))
    moves, places = [], []
    for z in range(0, n_chip, 2):
        for s in range(CORES):
            for i, y in enumerate((z, z + 1)):
                for m in masks:
                    put = [((2 * m + i) * piece, piece), (0, wide)]
                    taken = [((len(places), piece), piece), (0, wide)]
                    moves.append((None, m, taken, z + s, put))
                places.append((chip ^ y) * CORES + (core ^ s))
    exprs = collect(expr, moves, [(2 * n_cell * piece, wide)] * n_chip, jnp.stack(places))
    parts, gradient = [], None
    for z in range(0, n_chip, 2):
        pair = after(jnp.concatenate(own[z : z + 2], 1), *[swapped[m] for m in several])
        pieces = cell_gather(pair, 1)
        others = [squares, gradient] if z else []
        for half in (join(pieces, 1, others), join([core_swap(x) for x in pieces], 1)):
            added = jnp.dot(half, exprs[len(parts)], preferred_element_type=f32)
            gradient = added if gradient is None else gradient + added
            parts.append(half)

    step_size = 0.5 / (squares[0, 0] / (total_cells * factors) + EPSILON)
    own_blocks = lax.dynamic_slice_in_dim(block_mask, first_block(me_cell), wide_blocks, 0)
    support = jnp.repeat(own_blocks.T.astype(bf16), BLOCK, axis=0)
    spread = jnp.repeat(jnp.eye(wide_blocks, dtype=bf16), BLOCK, axis=1)
    support = jnp.dot(support, spread, preferred_element_type=f32)
    limit = step_size * LASSO * (1.0 - PRIOR_RELIEF * support)

    coefficient = shrink(step_size * (gradient / total_cells), limit, step_size)
    coefficient_bf = coefficient.astype(bf16)
    residuals = []
    for a, e in zip(parts, exprs):
        fitted = lax.dot_general(
            a, coefficient_bf, (((0,), (0,)), ((), ())), preferred_element_type=f32
        )
        residuals.append((fitted - e.astype(f32)).astype(bf16))

    tall = factors // n_cell
    arrived = {}
    for m in masks[::-1]:
        cut = lambda x: lax.dynamic_slice_in_dim(x, (me_cell ^ m) * tall, tall, 0)
        gradient = sum(
            jnp.dot(cut(a), b, preferred_element_type=f32) for a, b in zip(parts, residuals)
        )
        moved = cut(coefficient) - step_size * (gradient / total_cells)
        done = shrink(moved, cut(limit), step_size).astype(bf16)
        arrived[m] = done if m == 0 else cell_swap(done, m)
    stacked = jnp.stack([arrived[m] for m in masks])
    out = []
    for j in range(n_cell):
        block = lax.dynamic_index_in_dim(stacked, me_cell ^ j, 0, False)
        overlap = max(0, (j + 1) * wide_blocks - gene_blocks) * BLOCK
        out.append(block[:, overlap:])
    return jnp.concatenate(out, 1).astype(f32) * OUT_UNITS


def solution(mesh):
    in_specs = (P("cell", "gene"), P("gene", None), P("gene", None), P(None, "gene"))
    out_specs = P("cell", "gene")
    return jax.shard_map(
        on_device, mesh=mesh, in_specs=in_specs, out_specs=out_specs, check_vma=False
    )
```

```python
import jax
import jax.numpy as jnp
from jax import lax
from jax.experimental import pallas as pl
from jax.experimental.pallas import tpu as pltpu
from jax.sharding import PartitionSpec as P

BLOCK = 128
CORES = 2
ROWS = 16
SCOPED = 2 << 20
OUT_UNITS = 100.0
LASSO = 0.006
RIDGE = 0.1
PRIOR_RELIEF = 0.7
EPSILON = 1e-06

bf16, f32 = jnp.bfloat16, jnp.float32
ANYWHERE = pl.BlockSpec(memory_space=pl.ANY)


def shrink(moved, limit, step_size):
    kept = jnp.maximum(moved - limit, 0.0) - jnp.maximum(-moved - limit, 0.0)
    return kept / (1.0 + step_size * RIDGE)


def cell_swap(x, mask):
    n = lax.axis_size("cell")
    return lax.ppermute(x, "cell", [(i, i ^ mask) for i in range(n)])


def core_swap(x):
    n = lax.axis_size("gene")
    return lax.ppermute(x, "gene", [(i, i ^ 1) for i in range(n)])


def chip_swap(x, mask):
    n = lax.axis_size("gene")
    return lax.ppermute(x, "gene", [(i, i ^ (CORES * mask)) for i in range(n)])


def after(x, *others):
    return pl.pallas_call(
        lambda *refs: None,
        in_specs=[ANYWHERE] * (1 + len(others)),
        out_specs=ANYWHERE,
        out_shape=jax.ShapeDtypeStruct(x.shape, x.dtype),
        input_output_aliases={0: 0},
        compiler_params=pltpu.CompilerParams(vmem_limit_bytes=SCOPED),
        name="after",
    )(x, *others)


def collect(sources, moves, shapes, starts=None, others=(), apart=True):
    starts = jnp.zeros((1,), jnp.int32) if starts is None else starts.astype(jnp.int32)
    n, n_out = len(sources), len(shapes)

    def kernel(starts_ref, *refs):
        outs = refs[n + len(others) : n + len(others) + n_out]
        sems = refs[-1]

        def view(ref, slices):
            at = []
            for start, size in slices:
                if isinstance(start, tuple):
                    start = pl.multiple_of(starts_ref[start[0]] * start[1], start[1])
                at.append(pl.ds(start, size))
            return ref.at[tuple(at)]

        def copy(i):
            _, source, taken, out, put = moves[i]
            return pltpu.make_async_copy(view(refs[source], taken), view(outs[out], put), sems.at[i])

        def each(act):
            for i, (condition, *_) in enumerate(moves):
                if condition is None:
                    act(copy(i))
                else:
                    index, value = condition
                    pl.when(starts_ref[index] == value)(lambda i=i: act(copy(i)))

        each(lambda c: c.start())
        each(lambda c: c.wait())

    if apart:
        sources = [pltpu.with_memory_space_constraint(x, pltpu.HBM) for x in sources]
    return pl.pallas_call(
        kernel,
        in_specs=[pl.BlockSpec(memory_space=pltpu.SMEM)] + [ANYWHERE] * (n + len(others)),
        out_specs=[ANYWHERE] * n_out,
        out_shape=[pltpu.VMEM(shape, bf16) for shape in shapes],
        scratch_shapes=[pltpu.SemaphoreType.DMA((len(moves),))],
        compiler_params=pltpu.CompilerParams(vmem_limit_bytes=SCOPED),
        name="collect",
    )(starts, *sources, *others)


def join(columns, others=()):
    pieces = [x for column in columns for x in column]
    if any(x.shape[0] % ROWS or x.shape[1] % BLOCK for x in pieces):
        whole = jnp.concatenate([jnp.concatenate(column) for column in columns], 1)
        return after(whole, *others)
    moves, left = [], 0
    for column in columns:
        top = 0
        for x in column:
            height, width = x.shape
            put = [(top, height), (left, width)]
            moves.append((None, len(moves), [(0, height), (0, width)], 0, put))
            top += height
        left += width
    return collect(pieces, moves, [(top, left)], others=others)[0]


def masked_prior(prior_values, block_mask, others):
    gene_blocks, factor_blocks = block_mask.shape

    def kernel(mask_ref, prior_ref, *refs):
        out_ref, sems = refs[-2:]

        def copy(i):
            rows = pl.ds(pl.multiple_of(i * BLOCK, BLOCK), BLOCK)
            return pltpu.make_async_copy(prior_ref.at[rows], out_ref.at[rows], sems.at[i])

        @pl.loop(0, gene_blocks)
        def _(i):
            copy(i).start()

        @pl.loop(0, gene_blocks)
        def _(i):
            copy(i).wait()
            for j in range(factor_blocks):

                @pl.when(mask_ref[i, j] == 0)
                def _():
                    rows = pl.ds(pl.multiple_of(i * BLOCK, BLOCK), BLOCK)
                    out_ref[rows, j * BLOCK : (j + 1) * BLOCK] = jnp.zeros((BLOCK, BLOCK), bf16)

    return pl.pallas_call(
        kernel,
        in_specs=[pl.BlockSpec(memory_space=pltpu.SMEM)] + [ANYWHERE] * (1 + len(others)),
        out_specs=pl.BlockSpec(memory_space=pltpu.VMEM),
        out_shape=pltpu.VMEM(prior_values.shape, bf16),
        scratch_shapes=[pltpu.SemaphoreType.DMA((gene_blocks,))],
        compiler_params=pltpu.CompilerParams(vmem_limit_bytes=12 << 20),
        name="masked",
    )(block_mask, pltpu.with_memory_space_constraint(prior_values, pltpu.HBM), *others)


def sum_of_squares(x):
    def kernel(x_ref, out_ref):
        def step(i, total):
            part = x_ref[pl.ds(pl.multiple_of(i * ROWS, ROWS), ROWS), :].astype(f32)
            return total + part * part

        total = lax.fori_loop(
            0, x.shape[0] // ROWS, step, jnp.zeros((ROWS, x.shape[1]), f32), unroll=4
        )
        out_ref[...] = jnp.broadcast_to(jnp.sum(total, keepdims=True), out_ref.shape)

    return pl.pallas_call(
        kernel,
        in_specs=[pl.BlockSpec(memory_space=pltpu.VMEM)],
        out_specs=pl.BlockSpec(memory_space=pltpu.VMEM),
        out_shape=jax.ShapeDtypeStruct((8, BLOCK), f32),
        compiler_params=pltpu.CompilerParams(vmem_limit_bytes=8 << 20),
        name="squares",
    )(x)


def cell_gather(x, late=None):
    n = lax.axis_size("cell")
    half = x.shape[0] // 2
    got = {0: [x]}

    def half_of(pieces, i):
        if len(pieces) == 2:
            return pieces[i]
        part = pieces[0][i * half : (i + 1) * half]
        return after(part, *others) if others else part

    others = []
    for m in sorted(range(1, n), key=lambda m: m & (m - 1) != 0):
        low = m & -m
        high = m ^ low
        if not high:
            got[m] = [cell_swap(x, m)]
            continue
        if late and not others:
            others = late([pieces[0] for pieces in got.values()])
        first = cell_swap(half_of(got[high], 0), low)
        second = half_of(got[low], 1)
        for bit in range(n.bit_length()):
            if high >> bit & 1:
                second = cell_swap(second, 1 << bit)
        got[m] = [first, second]
    return [got[m] for m in range(n)]


def on_device(expression, prior_values, block_mask, gram_inverse):
    n_cell, n_gene = lax.axis_size("cell"), lax.axis_size("gene")
    n_chip = n_gene // CORES
    me_cell, me_gene = lax.axis_index("cell"), lax.axis_index("gene")
    chip, core = me_gene // CORES, me_gene % CORES
    cells, genes = expression.shape
    factors = prior_values.shape[1]
    gene_blocks, factor_blocks = block_mask.shape
    piece = cells // n_gene
    total_cells = cells * n_cell
    masks = list(range(n_cell))
    several = [m for m in masks if m & (m - 1)]
    single = [m for m in masks if m and m not in several]

    wide_blocks = -(-gene_blocks // n_cell)
    wide = wide_blocks * BLOCK

    def first_block(j):
        return jnp.minimum(j * wide_blocks, gene_blocks - wide_blocks)

    width = gram_inverse.shape[1]
    share = -(-width // (ROWS * n_cell)) * ROWS

    def share_start(j):
        return jnp.minimum(j * share, width - share)

    gram_share = lax.dynamic_slice_in_dim(gram_inverse.T, share_start(me_cell), share, 0)
    chip_order = [0]
    bits = [1 << i for i in reversed(range(n_chip.bit_length() - 1))]
    for bit in bits:
        chip_order += [z ^ bit for z in chip_order]

    def columns_of(starts, m):
        return lax.dynamic_slice_in_dim(expression, starts[m], wide, 1)

    starts = jnp.stack([first_block(me_cell ^ m) * BLOCK for m in masks]).astype(jnp.int32)
    columns = {m: columns_of(starts, m) for m in single}
    swapped = {m: cell_swap(columns[m], m) for m in single}

    masked = masked_prior(prior_values, block_mask, list(columns.values()))
    shares = gram_share
    for bit in bits[:-1]:
        shares = jnp.concatenate([shares, chip_swap(shares, bit)])

    def rows_of(core_index, others):
        moves = [
            (None, 0, [((z, piece), piece), (0, genes)], 0, [(z * piece, piece), (0, genes)])
            for z in range(n_chip)
        ]
        places = jnp.stack([z * CORES + core_index for z in range(n_chip)])
        return collect([expression], moves, [(n_chip * piece, genes)], places, others)[0]

    def scores_of(rows):
        return jnp.dot(rows, masked, preferred_element_type=f32)

    far_scores = scores_of(rows_of(core ^ 1, [shares])).astype(bf16)
    near_scores = scores_of(rows_of(core, [far_scores, *swapped.values()]))
    near_scores = lax.optimization_barrier(near_scores)
    shares = jnp.concatenate([shares, chip_swap(shares, 1)])
    from_core = core_swap(far_scores)

    def chip_scores(z):
        near, far = [
            lax.dynamic_slice_in_dim(x, (chip ^ z) * piece, piece, 0).astype(f32)
            for x in (near_scores, from_core)
        ]
        return near + far

    givens = [chip_scores(z).astype(bf16) for z in range(1, n_chip)]
    scores = chip_scores(0)
    got = {z: chip_swap(given, z) for z, given in zip(range(1, n_chip), givens)}
    for z in got:
        scores = scores + got[z].astype(f32)
    scores = scores.astype(bf16)

    shares = cell_gather(after(shares, *givens), lambda got: [scores])
    shares = [x for pieces in shares for x in pieces]
    near_gram = join([shares])
    starts = after(starts, *shares)
    columns.update({m: columns_of(starts, m) for m in [0] + several})
    swapped.update({m: cell_swap(columns[m], m) for m in several})
    far_gram = join([[core_swap(x) for x in shares]])
    halves = [
        lax.dot_general(
            gram, scores, (((1,), (1,)), ((), ())), preferred_element_type=f32
        ).astype(bf16)
        for gram in (near_gram, far_gram)
    ]
    moves, places = [], []
    for s in range(CORES):
        for m in masks:
            for i, z in enumerate(chip_order):
                from_row = (m * n_chip + i) * share
                j = me_cell ^ m
                first = ((chip ^ z) * CORES + (core ^ s)) * width
                at = len(places)
                places += [(first + j * share) // ROWS, j]
                for value in masks:
                    size = min(share, width - value * share)
                    if size > 0:
                        taken = [(from_row + share - size, size), (0, piece)]
                        moves.append(
                            ((at + 1, value), s, taken, 0, [((at, ROWS), size), (0, piece)])
                        )
    act = collect(halves, moves, [(factors, piece)], jnp.stack(places), apart=False)[0]

    own = [act]
    for z in range(1, n_chip):
        low = z & -z
        own.append(chip_swap(own[z ^ low], low))
    groups = [[z, z + 1] for z in range(0, n_chip, 2)]

    def expression_at(z, m, s):
        at = ((chip ^ z) * CORES + (core ^ s)) * piece
        return lax.dynamic_slice_in_dim(swapped[m] if m else columns[0], at, piece, 0)

    exprs, others_exprs = [], []
    for group in groups:
        near, far = [
            jnp.concatenate([expression_at(z, m, s) for z in group for m in masks]) for s in range(2)
        ]
        exprs.append(near)
        others_exprs.append(core_swap(far))

    gathered, parts, squares, gradients = [], [], [], ([], [])
    for z in range(n_chip):
        x = own[z]
        if z:
            x = after(x, *[gathered[-1][m][0] for m in single])
        if z == 1:
            x = after(x, *[swapped[m] for m in several])
        late = None
        if z == n_chip - 1:
            x = after(x, *[half for m in several for half in gathered[z - 2][m]])
            late = lambda got: [*squares, *gradients[0], *gradients[1]]
        gathered.append(cell_gather(x, late))
        if z % 2:
            parts.append(join([gathered[y][m] for y in groups[z // 2] for m in masks]))
            for total, some in zip(gradients, (exprs, others_exprs)):
                total.append(jnp.dot(parts[-1], some[z // 2], preferred_element_type=f32))
            squares.append(sum_of_squares(parts[-1]))
    gradient, other_gradient = [sum(total) for total in gradients]
    gradient = gradient + core_swap(other_gradient.astype(bf16)).astype(f32)
    squares = sum(squares)
    squares = squares + core_swap(squares)

    step_size = 0.5 / (squares[0, 0] / (total_cells * factors) + EPSILON)
    own_blocks = lax.dynamic_slice_in_dim(block_mask, first_block(me_cell), wide_blocks, 0)
    support = jnp.repeat(own_blocks.T.astype(bf16), BLOCK, axis=0)
    spread = jnp.repeat(jnp.eye(wide_blocks, dtype=bf16), BLOCK, axis=1)
    support = jnp.dot(support, spread, preferred_element_type=f32)
    limit = step_size * LASSO * (1.0 - PRIOR_RELIEF * support)

    coefficient = shrink(step_size * (gradient / total_cells), limit, step_size)
    coefficient_bf = coefficient.astype(bf16)

    def residuals_of(coefficient, some):
        out = []
        for a, e in zip(parts, some):
            fitted = lax.dot_general(
                a, coefficient, (((0,), (0,)), ((), ())), preferred_element_type=f32
            )
            out.append((fitted - e.astype(f32)).astype(bf16))
        return out

    residuals = residuals_of(coefficient_bf, exprs)
    others_residuals = residuals_of(core_swap(coefficient_bf), others_exprs)

    tall = factors // n_cell
    arrived = {}
    for m in masks[::-1]:
        cut = lambda x: lax.dynamic_slice_in_dim(x, (me_cell ^ m) * tall, tall, 0)
        gradient, other_gradient = [
            sum(jnp.dot(cut(a), b, preferred_element_type=f32) for a, b in zip(parts, some))
            for some in (residuals, others_residuals)
        ]
        gradient = gradient + core_swap(other_gradient.astype(bf16)).astype(f32)
        moved = cut(coefficient) - step_size * (gradient / total_cells)
        done = shrink(moved, cut(limit), step_size).astype(bf16)
        arrived[m] = done if m == 0 else cell_swap(done, m)
    stacked = jnp.stack([arrived[m] for m in masks])
    out = []
    for j in range(n_cell):
        block = lax.dynamic_index_in_dim(stacked, me_cell ^ j, 0, False)
        overlap = max(0, (j + 1) * wide_blocks - gene_blocks) * BLOCK
        out.append(block[:, overlap:])
    return jnp.concatenate(out, 1).astype(f32) * OUT_UNITS


def solution(mesh):
    in_specs = (P("cell", "gene"), P("gene", None), P("gene", None), P(None, "gene"))
    out_specs = P("cell", "gene")
    return jax.shard_map(
        on_device, mesh=mesh, in_specs=in_specs, out_specs=out_specs, check_vma=False
    )
```

```python
import jax
import jax.numpy as jnp
from jax import lax
from jax.experimental import pallas as pl
from jax.experimental.pallas import tpu as pltpu
from jax.sharding import PartitionSpec as P

BLOCK = 128
CORES = 2
ROWS = 16
SCOPED = 2 << 20
OUT_UNITS = 100.0
LASSO = 0.006
RIDGE = 0.1
PRIOR_RELIEF = 0.7
EPSILON = 1e-06

bf16, f32 = jnp.bfloat16, jnp.float32
ANYWHERE = pl.BlockSpec(memory_space=pl.ANY)


def shrink(moved, limit, step_size):
    kept = jnp.maximum(moved - limit, 0.0) - jnp.maximum(-moved - limit, 0.0)
    return kept / (1.0 + step_size * RIDGE)


def cell_swap(x, mask):
    n = lax.axis_size("cell")
    return lax.ppermute(x, "cell", [(i, i ^ mask) for i in range(n)])


def core_swap(x):
    n = lax.axis_size("gene")
    return lax.ppermute(x, "gene", [(i, i ^ 1) for i in range(n)])


def chip_swap(x, mask):
    n = lax.axis_size("gene")
    return lax.ppermute(x, "gene", [(i, i ^ (CORES * mask)) for i in range(n)])


def after(x, *others):
    return pl.pallas_call(
        lambda *refs: None,
        in_specs=[ANYWHERE] * (1 + len(others)),
        out_specs=ANYWHERE,
        out_shape=jax.ShapeDtypeStruct(x.shape, x.dtype),
        input_output_aliases={0: 0},
        compiler_params=pltpu.CompilerParams(vmem_limit_bytes=SCOPED),
        name="after",
    )(x, *others)


def collect(sources, moves, shapes, starts=None, others=(), apart=True):
    starts = jnp.zeros((1,), jnp.int32) if starts is None else starts.astype(jnp.int32)
    n, n_out = len(sources), len(shapes)

    def kernel(starts_ref, *refs):
        outs = refs[n + len(others) : n + len(others) + n_out]
        sems = refs[-1]

        def view(ref, slices):
            at = []
            for start, size in slices:
                if isinstance(start, tuple):
                    start = pl.multiple_of(starts_ref[start[0]] * start[1], start[1])
                at.append(pl.ds(start, size))
            return ref.at[tuple(at)]

        def copy(i):
            _, source, taken, out, put = moves[i]
            return pltpu.make_async_copy(view(refs[source], taken), view(outs[out], put), sems.at[i])

        def each(act):
            for i, (condition, *_) in enumerate(moves):
                if condition is None:
                    act(copy(i))
                else:
                    index, value = condition
                    pl.when(starts_ref[index] == value)(lambda i=i: act(copy(i)))

        each(lambda c: c.start())
        each(lambda c: c.wait())

    if apart:
        sources = [pltpu.with_memory_space_constraint(x, pltpu.HBM) for x in sources]
    return pl.pallas_call(
        kernel,
        in_specs=[pl.BlockSpec(memory_space=pltpu.SMEM)] + [ANYWHERE] * (n + len(others)),
        out_specs=[ANYWHERE] * n_out,
        out_shape=[pltpu.VMEM(shape, bf16) for shape in shapes],
        scratch_shapes=[pltpu.SemaphoreType.DMA((len(moves),))],
        compiler_params=pltpu.CompilerParams(vmem_limit_bytes=SCOPED),
        name="collect",
    )(starts, *sources, *others)


def join(columns, others=()):
    pieces = [x for column in columns for x in column]
    if any(x.shape[0] % ROWS or x.shape[1] % BLOCK for x in pieces):
        whole = jnp.concatenate([jnp.concatenate(column) for column in columns], 1)
        return after(whole, *others)
    moves, left = [], 0
    for column in columns:
        top = 0
        for x in column:
            height, width = x.shape
            put = [(top, height), (left, width)]
            moves.append((None, len(moves), [(0, height), (0, width)], 0, put))
            top += height
        left += width
    return collect(pieces, moves, [(top, left)], others=others)[0]


def masked_prior(prior_values, block_mask, others):
    gene_blocks, factor_blocks = block_mask.shape

    def kernel(mask_ref, prior_ref, *refs):
        out_ref, sems = refs[-2:]

        def copy(i):
            rows = pl.ds(pl.multiple_of(i * BLOCK, BLOCK), BLOCK)
            return pltpu.make_async_copy(prior_ref.at[rows], out_ref.at[rows], sems.at[i])

        @pl.loop(0, gene_blocks)
        def _(i):
            copy(i).start()

        @pl.loop(0, gene_blocks)
        def _(i):
            copy(i).wait()
            for j in range(factor_blocks):

                @pl.when(mask_ref[i, j] == 0)
                def _():
                    rows = pl.ds(pl.multiple_of(i * BLOCK, BLOCK), BLOCK)
                    out_ref[rows, j * BLOCK : (j + 1) * BLOCK] = jnp.zeros((BLOCK, BLOCK), bf16)

    return pl.pallas_call(
        kernel,
        in_specs=[pl.BlockSpec(memory_space=pltpu.SMEM)] + [ANYWHERE] * (1 + len(others)),
        out_specs=pl.BlockSpec(memory_space=pltpu.VMEM),
        out_shape=pltpu.VMEM(prior_values.shape, bf16),
        scratch_shapes=[pltpu.SemaphoreType.DMA((gene_blocks,))],
        compiler_params=pltpu.CompilerParams(vmem_limit_bytes=12 << 20),
        name="masked",
    )(block_mask, pltpu.with_memory_space_constraint(prior_values, pltpu.HBM), *others)


def sum_of_squares(x):
    def kernel(x_ref, out_ref):
        def step(i, total):
            part = x_ref[pl.ds(pl.multiple_of(i * ROWS, ROWS), ROWS), :].astype(f32)
            return total + part * part

        total = lax.fori_loop(
            0, x.shape[0] // ROWS, step, jnp.zeros((ROWS, x.shape[1]), f32), unroll=4
        )
        out_ref[...] = jnp.broadcast_to(jnp.sum(total, keepdims=True), out_ref.shape)

    return pl.pallas_call(
        kernel,
        in_specs=[pl.BlockSpec(memory_space=pltpu.VMEM)],
        out_specs=pl.BlockSpec(memory_space=pltpu.VMEM),
        out_shape=jax.ShapeDtypeStruct((8, BLOCK), f32),
        compiler_params=pltpu.CompilerParams(vmem_limit_bytes=8 << 20),
        name="squares",
    )(x)


def cell_gather(x, late=None):
    n = lax.axis_size("cell")
    half = x.shape[0] // 2
    got = {0: [x]}

    def half_of(pieces, i):
        if len(pieces) == 2:
            return pieces[i]
        part = pieces[0][i * half : (i + 1) * half]
        return after(part, *others) if others else part

    others = []
    for m in sorted(range(1, n), key=lambda m: m & (m - 1) != 0):
        low = m & -m
        high = m ^ low
        if not high:
            got[m] = [cell_swap(x, m)]
            continue
        if late and not others:
            others = late([pieces[0] for pieces in got.values()])
        first = cell_swap(half_of(got[high], 0), low)
        second = half_of(got[low], 1)
        for bit in range(n.bit_length()):
            if high >> bit & 1:
                second = cell_swap(second, 1 << bit)
        got[m] = [first, second]
    return [got[m] for m in range(n)]


def on_device(expression, prior_values, block_mask, gram_inverse):
    n_cell, n_gene = lax.axis_size("cell"), lax.axis_size("gene")
    n_chip = n_gene // CORES
    me_cell, me_gene = lax.axis_index("cell"), lax.axis_index("gene")
    chip, core = me_gene // CORES, me_gene % CORES
    cells, genes = expression.shape
    factors = prior_values.shape[1]
    gene_blocks, factor_blocks = block_mask.shape
    piece = cells // n_gene
    total_cells = cells * n_cell
    masks = list(range(n_cell))
    several = [m for m in masks if m & (m - 1)]
    single = [m for m in masks if m and m not in several]

    wide_blocks = -(-gene_blocks // n_cell)
    wide = wide_blocks * BLOCK

    def first_block(j):
        return jnp.minimum(j * wide_blocks, gene_blocks - wide_blocks)

    width = gram_inverse.shape[1]
    share = -(-width // (ROWS * n_cell)) * ROWS

    def share_start(j):
        return jnp.minimum(j * share, width - share)

    gram_share = lax.dynamic_slice_in_dim(gram_inverse.T, share_start(me_cell), share, 0)
    chip_order = [0]
    bits = [1 << i for i in reversed(range(n_chip.bit_length() - 1))]
    for bit in bits:
        chip_order += [z ^ bit for z in chip_order]

    def columns_of(starts, m):
        return lax.dynamic_slice_in_dim(expression, starts[m], wide, 1)

    starts = jnp.stack([first_block(me_cell ^ m) * BLOCK for m in masks]).astype(jnp.int32)
    columns = {m: columns_of(starts, m) for m in single}
    swapped = {m: cell_swap(columns[m], m) for m in single}

    masked = masked_prior(prior_values, block_mask, list(columns.values()))
    shares = gram_share
    for bit in bits[:-1]:
        shares = jnp.concatenate([shares, chip_swap(shares, bit)])

    def rows_of(core_index, others):
        moves = [
            (None, 0, [((z, piece), piece), (0, genes)], 0, [(z * piece, piece), (0, genes)])
            for z in range(n_chip)
        ]
        places = jnp.stack([z * CORES + core_index for z in range(n_chip)])
        return collect([expression], moves, [(n_chip * piece, genes)], places, others)[0]

    def scores_of(rows):
        return jnp.dot(rows, masked, preferred_element_type=f32)

    far_scores = scores_of(rows_of(core ^ 1, [shares])).astype(bf16)
    near_scores = scores_of(rows_of(core, [far_scores, *swapped.values()]))
    near_scores = lax.optimization_barrier(near_scores)
    shares = jnp.concatenate([shares, chip_swap(shares, 1)])
    from_core = core_swap(far_scores)

    def chip_scores(z):
        near, far = [
            lax.dynamic_slice_in_dim(x, (chip ^ z) * piece, piece, 0).astype(f32)
            for x in (near_scores, from_core)
        ]
        return near + far

    givens = [chip_scores(z).astype(bf16) for z in range(1, n_chip)]
    scores = chip_scores(0)
    got = {z: chip_swap(given, z) for z, given in zip(range(1, n_chip), givens)}
    for z in got:
        scores = scores + got[z].astype(f32)
    scores = scores.astype(bf16)

    shares = cell_gather(after(shares, *givens), lambda got: [scores])
    shares = [x for pieces in shares for x in pieces]
    starts = after(starts, *shares)
    columns.update({m: columns_of(starts, m) for m in [0] + several})
    swapped.update({m: cell_swap(columns[m], m) for m in several})
    sources = shares + [core_swap(x) for x in shares]
    sources = [
        lax.dot_general(
            gram, scores, (((1,), (1,)), ((), ())), preferred_element_type=f32
        ).astype(bf16)
        for gram in sources
    ]
    spots = [(i, row) for i, x in enumerate(shares) for row in range(x.shape[0])]
    moves, places = [], []
    for s in range(CORES):
        for m in masks:
            for i, z in enumerate(chip_order):
                source, row = spots[(m * n_chip + i) * share]
                j = me_cell ^ m
                first = ((chip ^ z) * CORES + (core ^ s)) * width
                at = len(places)
                places += [(first + j * share) // ROWS, j]
                for value in masks:
                    size = min(share, width - value * share)
                    if size > 0:
                        taken = [(row + share - size, size), (0, piece)]
                        put = [((at, ROWS), size), (0, piece)]
                        moves.append(((at + 1, value), s * len(shares) + source, taken, 0, put))
    act = collect(sources, moves, [(factors, piece)], jnp.stack(places), apart=False)[0]

    own = [act]
    for z in range(1, n_chip):
        low = z & -z
        own.append(chip_swap(own[z ^ low], low))
    groups = [[z, z + 1] for z in range(0, n_chip, 2)]

    def expression_at(z, m, s):
        at = ((chip ^ z) * CORES + (core ^ s)) * piece
        return lax.dynamic_slice_in_dim(swapped[m] if m else columns[0], at, piece, 0)

    exprs, others_exprs = [], []
    for group in groups:
        near, far = [
            jnp.concatenate([expression_at(z, m, s) for z in group for m in masks]) for s in range(2)
        ]
        exprs.append(near)
        others_exprs.append(core_swap(far))

    gathered, parts, squares, gradients = [], [], [], ([], [])
    for z in range(n_chip):
        x = own[z]
        if z:
            x = after(x, *[gathered[-1][m][0] for m in single])
        if z == 1:
            x = after(x, *[swapped[m] for m in several])
        late = None
        if z == n_chip - 1:
            x = after(x, *[half for m in several for half in gathered[z - 2][m]])
            late = lambda got: [*squares, *gradients[0], *gradients[1]]
        gathered.append(cell_gather(x, late))
        if z % 2:
            parts.append(join([gathered[y][m] for y in groups[z // 2] for m in masks]))
            for total, some in zip(gradients, (exprs, others_exprs)):
                total.append(jnp.dot(parts[-1], some[z // 2], preferred_element_type=f32))
            squares.append(sum_of_squares(parts[-1]))
    gradient, other_gradient = [sum(total) for total in gradients]
    gradient = gradient + core_swap(other_gradient.astype(bf16)).astype(f32)
    squares = sum(squares)
    squares = squares + core_swap(squares)

    step_size = 0.5 / (squares[0, 0] / (total_cells * factors) + EPSILON)
    own_blocks = lax.dynamic_slice_in_dim(block_mask, first_block(me_cell), wide_blocks, 0)
    support = jnp.repeat(own_blocks.T.astype(bf16), BLOCK, axis=0)
    spread = jnp.repeat(jnp.eye(wide_blocks, dtype=bf16), BLOCK, axis=1)
    support = jnp.dot(support, spread, preferred_element_type=f32)
    limit = step_size * LASSO * (1.0 - PRIOR_RELIEF * support)

    coefficient = shrink(step_size * (gradient / total_cells), limit, step_size)
    coefficient_bf = coefficient.astype(bf16)

    def residuals_of(coefficient, some):
        out = []
        for a, e in zip(parts, some):
            fitted = lax.dot_general(
                a, coefficient, (((0,), (0,)), ((), ())), preferred_element_type=f32
            )
            out.append((fitted - e.astype(f32)).astype(bf16))
        return out

    residuals = residuals_of(coefficient_bf, exprs)
    others_residuals = residuals_of(core_swap(coefficient_bf), others_exprs)

    tall = factors // n_cell
    arrived = {}
    for m in masks[::-1]:
        cut = lambda x: lax.dynamic_slice_in_dim(x, (me_cell ^ m) * tall, tall, 0)
        gradient, other_gradient = [
            sum(jnp.dot(cut(a), b, preferred_element_type=f32) for a, b in zip(parts, some))
            for some in (residuals, others_residuals)
        ]
        gradient = gradient + core_swap(other_gradient.astype(bf16)).astype(f32)
        moved = cut(coefficient) - step_size * (gradient / total_cells)
        done = shrink(moved, cut(limit), step_size).astype(bf16)
        if m in single:
            done = after(done, sent)
        sent = done
        arrived[m] = done if m == 0 else cell_swap(done, m)
    stacked = jnp.stack([arrived[m] for m in masks])
    out = []
    for j in range(n_cell):
        block = lax.dynamic_index_in_dim(stacked, me_cell ^ j, 0, False)
        overlap = max(0, (j + 1) * wide_blocks - gene_blocks) * BLOCK
        out.append(block[:, overlap:])
    return jnp.concatenate(out, 1).astype(f32) * OUT_UNITS


def solution(mesh):
    in_specs = (P("cell", "gene"), P("gene", None), P("gene", None), P(None, "gene"))
    out_specs = P("cell", "gene")
    return jax.shard_map(
        on_device, mesh=mesh, in_specs=in_specs, out_specs=out_specs, check_vma=False
    )
```

```python
import jax
import jax.numpy as jnp
from jax import lax
from jax.experimental import pallas as pl
from jax.experimental.pallas import tpu as pltpu
from jax.sharding import PartitionSpec as P

BLOCK = 128
CORES = 2
ROWS = 16
SCOPED = 2 << 20
OUT_UNITS = 100.0
LASSO = 0.006
RIDGE = 0.1
PRIOR_RELIEF = 0.7
EPSILON = 1e-06

bf16, f32 = jnp.bfloat16, jnp.float32
ANYWHERE = pl.BlockSpec(memory_space=pl.ANY)


def shrink(moved, limit, step_size):
    kept = jnp.maximum(moved - limit, 0.0) - jnp.maximum(-moved - limit, 0.0)
    return kept * (1.0 / (1.0 + step_size * RIDGE))


def cell_swap(x, mask):
    n = lax.axis_size("cell")
    return lax.ppermute(x, "cell", [(i, i ^ mask) for i in range(n)])


def core_swap(x):
    n = lax.axis_size("gene")
    return lax.ppermute(x, "gene", [(i, i ^ 1) for i in range(n)])


def chip_swap(x, mask):
    n = lax.axis_size("gene")
    return lax.ppermute(x, "gene", [(i, i ^ (CORES * mask)) for i in range(n)])


def after(x, *others):
    return pl.pallas_call(
        lambda *refs: None,
        in_specs=[ANYWHERE] * (1 + len(others)),
        out_specs=ANYWHERE,
        out_shape=jax.ShapeDtypeStruct(x.shape, x.dtype),
        input_output_aliases={0: 0},
        compiler_params=pltpu.CompilerParams(vmem_limit_bytes=SCOPED),
        name="after",
    )(x, *others)


def collect(sources, moves, shapes, starts=None, others=(), apart=True):
    starts = jnp.zeros((1,), jnp.int32) if starts is None else starts.astype(jnp.int32)
    n, n_out = len(sources), len(shapes)

    def kernel(starts_ref, *refs):
        outs = refs[n + len(others) : n + len(others) + n_out]
        sems = refs[-1]

        def view(ref, slices):
            at = []
            for start, size in slices:
                if isinstance(start, tuple):
                    start = pl.multiple_of(starts_ref[start[0]] * start[1], start[1])
                at.append(pl.ds(start, size))
            return ref.at[tuple(at)]

        def copy(i):
            _, source, taken, out, put = moves[i]
            return pltpu.make_async_copy(view(refs[source], taken), view(outs[out], put), sems.at[i])

        def each(act):
            for i, (condition, *_) in enumerate(moves):
                if condition is None:
                    act(copy(i))
                else:
                    index, value = condition
                    pl.when(starts_ref[index] == value)(lambda i=i: act(copy(i)))

        each(lambda c: c.start())
        each(lambda c: c.wait())

    if apart:
        sources = [pltpu.with_memory_space_constraint(x, pltpu.HBM) for x in sources]
    return pl.pallas_call(
        kernel,
        in_specs=[pl.BlockSpec(memory_space=pltpu.SMEM)] + [ANYWHERE] * (n + len(others)),
        out_specs=[ANYWHERE] * n_out,
        out_shape=[pltpu.VMEM(shape, bf16) for shape in shapes],
        scratch_shapes=[pltpu.SemaphoreType.DMA((len(moves),))],
        compiler_params=pltpu.CompilerParams(vmem_limit_bytes=SCOPED),
        name="collect",
    )(starts, *sources, *others)


def join(columns, others=()):
    pieces = [x for column in columns for x in column]
    if any(x.shape[0] % ROWS or x.shape[1] % BLOCK for x in pieces):
        whole = jnp.concatenate([jnp.concatenate(column) for column in columns], 1)
        return after(whole, *others)
    moves, left = [], 0
    for column in columns:
        top = 0
        for x in column:
            height, width = x.shape
            put = [(top, height), (left, width)]
            moves.append((None, len(moves), [(0, height), (0, width)], 0, put))
            top += height
        left += width
    return collect(pieces, moves, [(top, left)], others=others)[0]


def masked_prior(prior_values, block_mask, others):
    gene_blocks, factor_blocks = block_mask.shape

    def kernel(mask_ref, prior_ref, *refs):
        out_ref, sems = refs[-2:]

        def copy(i):
            rows = pl.ds(pl.multiple_of(i * BLOCK, BLOCK), BLOCK)
            return pltpu.make_async_copy(prior_ref.at[rows], out_ref.at[rows], sems.at[i])

        @pl.loop(0, gene_blocks)
        def _(i):
            copy(i).start()

        @pl.loop(0, gene_blocks)
        def _(i):
            copy(i).wait()
            for j in range(factor_blocks):

                @pl.when(mask_ref[i, j] == 0)
                def _():
                    rows = pl.ds(pl.multiple_of(i * BLOCK, BLOCK), BLOCK)
                    out_ref[rows, j * BLOCK : (j + 1) * BLOCK] = jnp.zeros((BLOCK, BLOCK), bf16)

    return pl.pallas_call(
        kernel,
        in_specs=[pl.BlockSpec(memory_space=pltpu.SMEM)] + [ANYWHERE] * (1 + len(others)),
        out_specs=pl.BlockSpec(memory_space=pltpu.VMEM),
        out_shape=pltpu.VMEM(prior_values.shape, bf16),
        scratch_shapes=[pltpu.SemaphoreType.DMA((gene_blocks,))],
        compiler_params=pltpu.CompilerParams(vmem_limit_bytes=12 << 20),
        name="masked",
    )(block_mask, pltpu.with_memory_space_constraint(prior_values, pltpu.HBM), *others)


def sum_of_squares(x):
    def kernel(x_ref, out_ref):
        def step(i, total):
            part = x_ref[pl.ds(pl.multiple_of(i * ROWS, ROWS), ROWS), :].astype(f32)
            return total + part * part

        total = lax.fori_loop(
            0, x.shape[0] // ROWS, step, jnp.zeros((ROWS, x.shape[1]), f32), unroll=4
        )
        out_ref[...] = jnp.broadcast_to(jnp.sum(total, keepdims=True), out_ref.shape)

    return pl.pallas_call(
        kernel,
        in_specs=[pl.BlockSpec(memory_space=pltpu.VMEM)],
        out_specs=pl.BlockSpec(memory_space=pltpu.VMEM),
        out_shape=jax.ShapeDtypeStruct((8, BLOCK), f32),
        compiler_params=pltpu.CompilerParams(vmem_limit_bytes=8 << 20),
        name="squares",
    )(x)


def cell_gather(x, late=None):
    n = lax.axis_size("cell")
    half = x.shape[0] // 2
    got = {0: [x]}

    def half_of(pieces, i):
        if len(pieces) == 2:
            return pieces[i]
        part = pieces[0][i * half : (i + 1) * half]
        return after(part, *others) if others else part

    others = []
    for m in sorted(range(1, n), key=lambda m: m & (m - 1) != 0):
        low = m & -m
        high = m ^ low
        if not high:
            got[m] = [cell_swap(x, m)]
            continue
        if late and not others:
            others = late([pieces[0] for pieces in got.values()])
        first = cell_swap(half_of(got[high], 0), low)
        second = half_of(got[low], 1)
        for bit in range(n.bit_length()):
            if high >> bit & 1:
                second = cell_swap(second, 1 << bit)
        got[m] = [first, second]
    return [got[m] for m in range(n)]


def on_device(expression, prior_values, block_mask, gram_inverse):
    n_cell, n_gene = lax.axis_size("cell"), lax.axis_size("gene")
    n_chip = n_gene // CORES
    me_cell, me_gene = lax.axis_index("cell"), lax.axis_index("gene")
    chip, core = me_gene // CORES, me_gene % CORES
    cells, genes = expression.shape
    factors = prior_values.shape[1]
    gene_blocks, factor_blocks = block_mask.shape
    piece = cells // n_gene
    total_cells = cells * n_cell
    masks = list(range(n_cell))
    several = [m for m in masks if m & (m - 1)]
    single = [m for m in masks if m and m not in several]

    wide_blocks = -(-gene_blocks // n_cell)
    wide = wide_blocks * BLOCK

    def first_block(j):
        return jnp.minimum(j * wide_blocks, gene_blocks - wide_blocks)

    width = gram_inverse.shape[1]
    share = -(-width // (ROWS * n_cell)) * ROWS

    def share_start(j):
        return jnp.minimum(j * share, width - share)

    gram_share = lax.dynamic_slice_in_dim(gram_inverse.T, share_start(me_cell), share, 0)
    chip_order = [0]
    bits = [1 << i for i in reversed(range(n_chip.bit_length() - 1))]
    for bit in bits:
        chip_order += [z ^ bit for z in chip_order]

    def columns_of(starts, m):
        return lax.dynamic_slice_in_dim(expression, starts[m], wide, 1)

    starts = jnp.stack([first_block(me_cell ^ m) * BLOCK for m in masks]).astype(jnp.int32)
    columns = {m: columns_of(starts, m) for m in single}
    swapped = {m: cell_swap(columns[m], m) for m in single}

    masked = masked_prior(prior_values, block_mask, list(columns.values()))
    shares = gram_share
    for bit in bits[:-1]:
        shares = jnp.concatenate([shares, chip_swap(shares, bit)])

    def rows_of(core_index, others):
        moves = [
            (None, 0, [((z, piece), piece), (0, genes)], 0, [(z * piece, piece), (0, genes)])
            for z in range(n_chip)
        ]
        places = jnp.stack([z * CORES + core_index for z in range(n_chip)])
        return collect([expression], moves, [(n_chip * piece, genes)], places, others)[0]

    def scores_of(rows):
        return jnp.dot(rows, masked, preferred_element_type=f32)

    far_scores = scores_of(rows_of(core ^ 1, [shares])).astype(bf16)
    near_scores = scores_of(rows_of(core, [far_scores, *swapped.values()]))
    near_scores = lax.optimization_barrier(near_scores)
    shares = jnp.concatenate([shares, chip_swap(shares, 1)])
    from_core = core_swap(far_scores)

    def chip_scores(z):
        near, far = [
            lax.dynamic_slice_in_dim(x, (chip ^ z) * piece, piece, 0).astype(f32)
            for x in (near_scores, from_core)
        ]
        return near + far

    givens = [chip_scores(z).astype(bf16) for z in range(1, n_chip)]
    scores = chip_scores(0)
    got = {z: chip_swap(given, z) for z, given in zip(range(1, n_chip), givens)}
    for z in got:
        scores = scores + got[z].astype(f32)
    scores = scores.astype(bf16)

    shares = cell_gather(after(shares, *givens), lambda got: [scores])
    shares = [x for pieces in shares for x in pieces]
    starts = after(starts, *shares)
    columns.update({m: columns_of(starts, m) for m in several})
    swapped.update({m: cell_swap(columns[m], m) for m in several})
    columns[0] = columns_of(after(starts, *[swapped[m] for m in several]), 0)
    sources = shares + [core_swap(x) for x in shares]
    sources = [
        lax.dot_general(
            gram, scores, (((1,), (1,)), ((), ())), preferred_element_type=f32
        ).astype(bf16)
        for gram in sources
    ]
    spots = [(i, row) for i, x in enumerate(shares) for row in range(x.shape[0])]
    moves, places = [], []
    for s in range(CORES):
        for m in masks:
            for i, z in enumerate(chip_order):
                source, row = spots[(m * n_chip + i) * share]
                j = me_cell ^ m
                first = ((chip ^ z) * CORES + (core ^ s)) * width
                at = len(places)
                places += [(first + j * share) // ROWS, j]
                for value in masks:
                    size = min(share, width - value * share)
                    if size > 0:
                        taken = [(row + share - size, size), (0, piece)]
                        put = [((at, ROWS), size), (0, piece)]
                        moves.append(((at + 1, value), s * len(shares) + source, taken, 0, put))
    act = collect(sources, moves, [(factors, piece)], jnp.stack(places), apart=False)[0]

    own = [act]
    for z in range(1, n_chip):
        low = z & -z
        own.append(chip_swap(own[z ^ low], low))
    groups = [[z, z + 1] for z in range(0, n_chip, 2)]

    def expression_at(z, m, s):
        at = ((chip ^ z) * CORES + (core ^ s)) * piece
        return lax.dynamic_slice_in_dim(swapped[m] if m else columns[0], at, piece, 0)

    exprs, others_exprs = [], []
    for group in groups:
        near, far = [
            jnp.concatenate([expression_at(z, m, s) for z in group for m in masks]) for s in range(2)
        ]
        exprs.append(near)
        others_exprs.append(core_swap(far))

    gathered, parts, squares, gradients = [], [], [], ([], [])
    for z in range(n_chip):
        x = own[z]
        if z:
            x = after(x, *[gathered[-1][m][0] for m in single])
        if z == 1:
            x = after(x, *[swapped[m] for m in several])
        late = None
        if z == n_chip - 1:
            x = after(x, *[half for m in several for half in gathered[z - 2][m]])
            done = [x[:8, :BLOCK] for x in (*gradients[0], *gradients[1])]
            late = lambda got: [*squares, *done]
        gathered.append(cell_gather(x, late))
        if z % 2:
            parts.append(join([gathered[y][m] for y in groups[z // 2] for m in masks]))
            for total, some in zip(gradients, (exprs, others_exprs)):
                total.append(jnp.dot(parts[-1], some[z // 2], preferred_element_type=f32))
            squares.append(sum_of_squares(parts[-1]))
    gradient, other_gradient = [sum(total) for total in gradients]
    gradient = gradient + core_swap(other_gradient.astype(bf16)).astype(f32)
    squares = sum(squares)
    squares = squares + core_swap(squares)

    step_size = 0.5 / (squares[0, 0] / (total_cells * factors) + EPSILON)
    own_blocks = lax.dynamic_slice_in_dim(block_mask, first_block(me_cell), wide_blocks, 0)
    support = jnp.repeat(own_blocks.T.astype(bf16), BLOCK, axis=0)
    spread = jnp.repeat(jnp.eye(wide_blocks, dtype=bf16), BLOCK, axis=1)
    support = jnp.dot(support, spread, preferred_element_type=f32)
    limit = step_size * LASSO * (1.0 - PRIOR_RELIEF * support)

    coefficient = shrink(step_size * (gradient / total_cells), limit, step_size)
    coefficient_bf = coefficient.astype(bf16)

    def residuals_of(coefficient, some):
        out = []
        for a, e in zip(parts, some):
            fitted = lax.dot_general(
                a, coefficient, (((0,), (0,)), ((), ())), preferred_element_type=f32
            )
            out.append((fitted - e.astype(f32)).astype(bf16))
        return out

    residuals = residuals_of(coefficient_bf, exprs)
    others_residuals = residuals_of(core_swap(coefficient_bf), others_exprs)

    tall = factors // n_cell
    arrived = {}
    for m in masks[::-1]:
        cut = lambda x: lax.dynamic_slice_in_dim(x, (me_cell ^ m) * tall, tall, 0)
        gradient, other_gradient = [
            sum(jnp.dot(cut(a), b, preferred_element_type=f32) for a, b in zip(parts, some))
            for some in (residuals, others_residuals)
        ]
        gradient = gradient + core_swap(other_gradient.astype(bf16)).astype(f32)
        moved = cut(coefficient) - step_size * (gradient / total_cells)
        done = shrink(moved, cut(limit), step_size).astype(bf16)
        if m in single:
            done = after(done, sent)
        sent = done
        arrived[m] = done if m == 0 else cell_swap(done, m)
    stacked = jnp.stack([arrived[m] for m in masks])
    out = []
    for j in range(n_cell):
        block = lax.dynamic_index_in_dim(stacked, me_cell ^ j, 0, False)
        overlap = max(0, (j + 1) * wide_blocks - gene_blocks) * BLOCK
        out.append(block[:, overlap:])
    return jnp.concatenate(out, 1).astype(f32) * OUT_UNITS


def solution(mesh):
    in_specs = (P("cell", "gene"), P("gene", None), P("gene", None), P(None, "gene"))
    out_specs = P("cell", "gene")
    return jax.shard_map(
        on_device, mesh=mesh, in_specs=in_specs, out_specs=out_specs, check_vma=False
    )
```
